512 devices in a mesh: ctx: 32 (over y, z_lo, core), tp: 4 (over z_hi), dp: 4 (over x).
Axes of the slice: x: 4, y: 8, z: 8 (z_hi: 4, z_lo: 2; z = z_hi * 2 + z_lo), core: 2. Of those that a mesh axis runs over, the one named last changes fastest.
Arguments:
- queries: bfloat16 [16384, 8192], P(('dp', 'ctx'), 'tp'), parts along dimension 0
- keys: bfloat16 [16384, 1024], P(('dp', 'ctx'), 'tp'), parts along dimension 0
- values: bfloat16 [16384, 1024], P(('dp', 'ctx'), 'tp'), parts along dimension 0, may hold values from -6 to 6
- loader_pos: int32 [16384], P(('dp', 'ctx')), parts along dimension 0, may hold values from 0 to 4095, as said below
- reset_pos: int32 [16384], P(('dp', 'ctx')), parts along dimension 0, may hold values from 0 to 2047, as said below
- doc_starts: int32 [64], P('dp'), parts along dimension 0, may hold values from 0 to 4095, as said below
Outputs:
- attention: bfloat16 [16384, 8192], P(('dp', 'ctx'), 'tp'), parts along dimension 0
The draws below stay inside these ranges and needn't reach their ends.
There are 4 independent parts, one for each index of `dp`. The reference program is written for one: setup_inputs(seed, part) draws one part's arguments, and reference() takes and returns one part's arrays. A program takes and returns all parts, laid end to end along the dimension named above; each array names one. Nothing has to cross between parts.
Inputs may be any that keep to these rules, and one draw needn't show every extreme that they name: `loader_pos`: a permutation of the 4096 positions; split the positions into 64 blocks of 64 and let shard i own blocks i and 63 - i: the rows of each device of ctx hold exactly 4 positions owned by each shard. `reset_pos`: the position of each loader row's token within its document, loader_pos minus the start of its document. `doc_starts`: increasing, the first 0; every document has 1 to 2048 tokens and one has exactly 2048.
All inputs are finite; a program needn't handle non-finite values.
Results may differ from the reference program's by a relative error of at most 0.006.
Values may be sent and summed in bfloat16 or wider, within the bound.
A program may use at most 64 MiB of HBM per device.

```python
import math
import jax
import jax.numpy as jnp
from jax import lax

QUERY_HEADS = 64
KEY_VALUE_HEADS = 8
HEAD_WIDTH = 128
TOK_DEV = 128
PACKED_TOKENS = 4096
NDOC = 16
MOST = 2048
N_CTX = 32


def shared_keys(key):
    return jax.random.normal(jax.random.fold_in(key, 101), (PACKED_TOKENS, KEY_VALUE_HEADS, HEAD_WIDTH), jnp.float32)


def document_starts(key):
    key = jax.random.fold_in(key, 202)
    key_one, key_two = jax.random.split(key)
    remaining = PACKED_TOKENS - MOST
    cut_points = jnp.sort(jax.random.permutation(key_one, remaining - 1)[:NDOC - 2] + 1).astype(jnp.int32)
    edge_list = jnp.concatenate([jnp.zeros((1,), jnp.int32), cut_points, jnp.full((1,), remaining, jnp.int32)])
    others = edge_list[1:] - edge_list[:-1]
    long_slot = jax.random.randint(key_two, (), 0, NDOC)
    slot_index = jnp.arange(NDOC)
    earlier_len = others[jnp.clip(slot_index, 0, NDOC - 2)]
    later_len = others[jnp.clip(slot_index - 1, 0, NDOC - 2)]
    lengths = jnp.where(slot_index < long_slot, earlier_len, jnp.where(slot_index == long_slot, MOST, later_len)).astype(jnp.int32)
    return (jnp.cumsum(lengths) - lengths).astype(jnp.int32)


def loader_positions(key):
    key = jax.random.fold_in(key, 303)
    key_one, key_two = jax.random.split(key)
    half_rows = TOK_DEV // 2
    shard_ids = jnp.arange(N_CTX)[:, None]
    offsets = jnp.arange(TOK_DEV)[None, :]
    block_of = jnp.where(offsets < half_rows, shard_ids, 2 * N_CTX - 1 - shard_ids)
    owned_pos = (block_of * half_rows + offsets % half_rows).astype(jnp.int32)
    shuffled = jax.random.permutation(key_one, owned_pos, axis=1, independent=True)
    regroup = jnp.transpose(shuffled.reshape(N_CTX, N_CTX, TOK_DEV // N_CTX), (1, 0, 2)).reshape(N_CTX, TOK_DEV)
    return jax.random.permutation(key_two, regroup, axis=1, independent=True).reshape(PACKED_TOKENS).astype(jnp.int32)


def draw_queries(key, part):
    key = jax.random.fold_in(key, 1)
    key_one = jax.random.fold_in(key, 0)
    drawn = jax.random.normal(key_one, (PACKED_TOKENS, QUERY_HEADS, HEAD_WIDTH), jnp.float32)
    return drawn.reshape(PACKED_TOKENS, QUERY_HEADS * HEAD_WIDTH).astype(jnp.bfloat16)


def draw_keys(key, part):
    key_base_offset = shared_keys(key)
    return key_base_offset.reshape(PACKED_TOKENS, KEY_VALUE_HEADS * HEAD_WIDTH).astype(jnp.bfloat16)


def draw_loader_pos(key, part):
    return loader_positions(key)


def draw_reset_pos(key, part):
    starts = document_starts(key)
    at_rows = loader_positions(key)
    doc_index = jnp.sum((starts[None, :] <= at_rows[:, None]).astype(jnp.int32), axis=1, dtype=jnp.int32) - 1
    return (at_rows - starts[doc_index]).astype(jnp.int32)


def draw_doc_starts(key, part):
    return document_starts(key)


def shard_levels(own_key, dims, cuts, low, largest):
    def one(dim, shards_of):
        draws = jax.random.uniform(jax.random.fold_in(jax.random.fold_in(own_key, 6), dim), (shards_of,), jnp.float32, low / len(cuts), largest / len(cuts))
        return jnp.repeat(jnp.exp(draws), dims[dim] // shards_of).reshape((-1,) + (1,) * (len(dims) - dim - 1))

    loudness = one(*cuts[0])
    for cut in cuts[1:]:
        loudness = loudness * one(*cut)
    return loudness


def noise(key, shape, spread, bound, pieces=(), kind=jnp.bfloat16):
    factor_of = shard_levels(key, shape, pieces, -0.22, 0.18) if pieces else 1.0
    entries = jax.random.normal(key, shape, jnp.float32) * spread * factor_of
    return jnp.minimum(jnp.maximum(entries, -bound), bound).astype(kind)


def setup_inputs(seed: int = 0, part: int = 0) -> dict:
    seeds = jax.random.split(jax.random.key(seed), 7)
    own_keys = jax.random.split(jax.random.fold_in(seeds[6], part), 7)
    queries = draw_queries(jax.random.fold_in(jax.random.fold_in(seeds[6], part), 71), part)
    keys = draw_keys(jax.random.fold_in(jax.random.fold_in(seeds[6], part), 71), part)
    values = noise(own_keys[2], (PACKED_TOKENS, KEY_VALUE_HEADS * HEAD_WIDTH), 1.0, 6.0, ((0, 32), (1, 4)))
    loader_pos = draw_loader_pos(jax.random.fold_in(jax.random.fold_in(seeds[6], part), 71), part)
    reset_pos = draw_reset_pos(jax.random.fold_in(jax.random.fold_in(seeds[6], part), 71), part)
    doc_starts = draw_doc_starts(jax.random.fold_in(jax.random.fold_in(seeds[6], part), 71), part)
    return {"queries": queries, "keys": keys, "values": values, "loader_pos": loader_pos, "reset_pos": reset_pos, "doc_starts": doc_starts}


ROPE_BASE = 1000000.0

def rotate(row_block, positions):
    row_count = row_block.shape[0]
    q_heads = row_block.shape[1] // HEAD_WIDTH
    lanes = row_block.astype(jnp.float32).reshape(row_count, q_heads, HEAD_WIDTH)
    frequency = ROPE_BASE ** (-jnp.arange(HEAD_WIDTH // 2, dtype=jnp.float32) * 2.0 / HEAD_WIDTH)
    angles = positions.astype(jnp.float32)[:, None] * frequency[None, :]
    cosine = jnp.cos(angles)[:, None, :]
    sine_term = jnp.sin(angles)[:, None, :]
    lower_half = lanes[..., :HEAD_WIDTH // 2]
    upper_half = lanes[..., HEAD_WIDTH // 2:]
    result = jnp.concatenate([lower_half * cosine - upper_half * sine_term, upper_half * cosine + lower_half * sine_term], axis=-1)
    return result.reshape(row_count, q_heads * HEAD_WIDTH).astype(jnp.bfloat16)

def document_of(positions, doc_starts):
    return lax.optimization_barrier(jnp.sum((doc_starts[None, :] <= positions[:, None]).astype(jnp.int32), axis=1, dtype=jnp.int32)) - 1

def reference(queries, keys, values, loader_pos, reset_pos, doc_starts):
    q_rot = rotate(queries, reset_pos)
    k_rot = rotate(keys, reset_pos)
    seq_order = jnp.argsort(loader_pos)
    query_sequence = q_rot[seq_order]
    key_sequence = k_rot[seq_order]
    value_sequence = values[seq_order]
    positions = jnp.arange(PACKED_TOKENS, dtype=jnp.int32)
    doc_ids = document_of(positions, doc_starts)
    heads_per_group = QUERY_HEADS // KEY_VALUE_HEADS
    query_block = math.gcd(PACKED_TOKENS, 512)
    count_of_blocks = PACKED_TOKENS // query_block
    score_scale = 1.0 / math.sqrt(HEAD_WIDTH)
    query_grouped = jnp.moveaxis(query_sequence.reshape(count_of_blocks, query_block, KEY_VALUE_HEADS, heads_per_group, HEAD_WIDTH), 2, 0)
    key_grouped = jnp.moveaxis(key_sequence.reshape(PACKED_TOKENS, KEY_VALUE_HEADS, HEAD_WIDTH), 1, 0)
    value_grouped = jnp.moveaxis(value_sequence.reshape(PACKED_TOKENS, KEY_VALUE_HEADS, HEAD_WIDTH), 1, 0)
    pos_blocks = positions.reshape(count_of_blocks, query_block)
    doc_blocks = doc_ids.reshape(count_of_blocks, query_block)

    def one_group(group_args):
        q_group, k_group, v_group = group_args
        k_float = k_group.astype(jnp.float32)
        v_float = v_group.astype(jnp.float32)

        def one_block(block_args):
            q_part, q_pos, q_doc = block_args
            scores = jnp.einsum('tjd,kd->jtk', q_part.astype(jnp.float32), k_float) * score_scale
            allowed = (q_doc[:, None] == doc_ids[None, :]) & (positions[None, :] <= q_pos[:, None])
            scores = jnp.where(allowed[None], scores, -1e+30)
            maxima = lax.optimization_barrier(jnp.max(scores, axis=-1, keepdims=True))
            weights = jnp.where(allowed[None], jnp.exp(scores - maxima), 0.0).astype(jnp.bfloat16)
            totals = lax.optimization_barrier(jnp.sum(weights.astype(jnp.float32), axis=-1))
            summed = jnp.einsum('jtk,kd->tjd', weights.astype(jnp.float32), v_float)
            return summed / jnp.transpose(totals)[:, :, None]
        return lax.map(one_block, (q_group, pos_blocks, doc_blocks)).reshape(PACKED_TOKENS, heads_per_group, HEAD_WIDTH)
    grouped = lax.map(one_group, (query_grouped, key_grouped, value_grouped))
    out_seq = jnp.transpose(grouped, (1, 0, 2, 3)).reshape(PACKED_TOKENS, QUERY_HEADS * HEAD_WIDTH)
    return out_seq[loader_pos].astype(jnp.bfloat16)
```

```python
import functools
import math

import jax
import jax.numpy as jnp
import numpy as np
from jax import lax
from jax.experimental import pallas as pl
from jax.experimental.pallas import tpu as pltpu
from jax.sharding import PartitionSpec as P

MESH = pl.DeviceIdType.MESH
HEAD_WIDTH = 128
HALF = HEAD_WIDTH // 2
ROPE_BASE = 1000000.0
SCALE = math.log2(math.e) / math.sqrt(HEAD_WIDTH)
ROWS = 128
GROUP = 8
COLS = GROUP * ROWS
NY = 8
UNIT = 512
MASKED = -1e30
SUB_ROWS = ((0, 256), (256, 272))
ITEM_ROWS = 528

PLAN = {
    "edges": [
        (0, (0, 1), (0, 0)), (0, (1, 0), (0, 0)), (0, (-1, 0), (0, 0)), (0, (1, 1), (1, 0)), (0, (-1, 1), (-1, 0)),
        (0, (2, 0), (1, 0)), (0, (-2, 0), (-1, 0)), (0, (2, 1), (2, 0)), (0, (-2, 1), (-2, 0)), (0, (3, 0), (2, 0)),
        (0, (-3, 0), (-2, 0)), (0, (3, 1), (3, 0)), (0, (-3, 1), (-3, 0)), (0, (4, 0), (3, 0)), (0, (4, 1), (3, 1)),
        (1, (0, 1), (0, 0)), (1, (1, 0), (0, 0)), (1, (-1, 0), (0, 0)), (1, (1, 1), (0, 1)), (1, (-1, 1), (0, 1)),
        (1, (2, 0), (1, 0)), (1, (-2, 0), (-1, 0)), (1, (2, 1), (1, 1)), (1, (-2, 1), (-1, 1)), (1, (3, 0), (2, 0)),
        (1, (-3, 0), (-2, 0)), (1, (3, 1), (2, 1)), (1, (-3, 1), (-2, 1)), (1, (-4, 0), (-3, 0)),
        (1, (-4, 1), (-4, 0)),
    ],
    "waits": [
        (0, (0, 1)), (0, (1, 0)), (0, (-1, 0)), (1, (0, 1)), (1, (1, 0)), (1, (-1, 0)), (0, (1, 1)), (0, (2, 0)),
        (0, (-2, 0)), (0, (-1, 1)), (1, (1, 1)), (1, (-2, 0)), (1, (-1, 1)), (1, (2, 0)), (0, (2, 1)), (0, (-2, 1)),
        (0, (-3, 0)), (0, (3, 0)), (1, (2, 1)), (1, (-3, 0)), (1, (-2, 1)), (1, (3, 0)), (0, (-3, 1)), (0, (3, 1)),
        (0, (4, 0)), (1, (-4, 0)), (1, (3, 1)), (1, (-3, 1)), (0, (4, 1)), (1, (-4, 1)),
    ],
    "steps": [
        [(0, 0)], [(0, 1), (1, 0)], [(-1, 0), (1, 1)], [(-2, 0), (-1, 1)], [(2, 0), (2, 1)], [(-3, 0), (-2, 1)],
        [(3, 0), (4, 0)], [(3, 1), (-3, 1)], [(4, 1)],
    ],
    "before": [
        0, 0, 0, 0, 6, 6, 6, 6, 11, 11, 12, 14, 16, 18, 18, 18, 19, 20, 22, 22, 25, 25, 25, 27, 28, 28, 28, 29, 29,
        29, 30, 30, 30, 30, 30, 30,
    ],
}


def sine_cosine(angle):
    turn = jnp.floor(angle * (2.0 / math.pi) + 0.5)
    rest = ((angle - turn * 1.5703125) - turn * 4.837512969970703125e-4) - turn * 7.54978995489188216e-8
    square = rest * rest
    sine = ((-1.9515295891e-4 * square + 8.3321608736e-3) * square - 1.6666654611e-1) * square * rest + rest
    cosine = (
        (2.443315711809948e-5 * square - 1.388731625493765e-3) * square + 4.166664568298827e-2
    ) * square * square - 0.5 * square + 1.0
    quarter = turn.astype(jnp.int32)
    swap = (quarter & 1) == 1
    sine_out = jnp.where(swap, cosine, sine)
    cosine_out = jnp.where(swap, sine, cosine)
    sine_out = jnp.where((quarter & 2) == 2, -sine_out, sine_out)
    cosine_out = jnp.where(((quarter + 1) & 2) == 2, -cosine_out, cosine_out)
    return sine_out, cosine_out


def kernel(
    q_hbm, k_hbm, v_hbm, pos_hbm, reset_hbm, freq_hbm, out_hbm,
    q_in, k_in, v_in, pos_in, reset_in, freq_in,
    items, stage, q_t, q_stage, place, place_sib, bounds, mask, top, total, acc, out_buf,
    in_sem, item_sem, sib_sem, send_sem, out_sem,
):
    ctx = lax.axis_index("ctx")
    tp = lax.axis_index("tp")
    dp = lax.axis_index("dp")
    y, z, core = ctx // 4, (ctx // 2) % 2, ctx % 2

    def device(yy, zz, cc):
        return ((yy * 2 + zz) * 2 + cc, tp, dp)

    def around(yy):
        return lax.rem(yy + 2 * NY, NY)

    sibling = device(y, z, 1 - core)

    barrier = pltpu.get_barrier_semaphore()
    for other in (
        device(around(y + 1), z, core), device(around(y - 1), z, core), device(y, 1 - z, core), sibling,
    ):
        pl.semaphore_signal(barrier, inc=1, device_id=other, device_id_type=MESH)

    def head_cols(slot, width):
        head = core if slot == 0 else 1 - core
        return pl.ds(pl.multiple_of(head * width, width), width)

    loads = [
        pltpu.make_async_copy(pos_hbm, pos_in, in_sem.at[0]),
        pltpu.make_async_copy(reset_hbm, reset_in, in_sem.at[1]),
        pltpu.make_async_copy(freq_hbm, freq_in, in_sem.at[2]),
    ]
    for slot in (1, 0):
        loads.append(pltpu.make_async_copy(k_hbm.at[:, head_cols(slot, HEAD_WIDTH)], k_in.at[slot], in_sem.at[3 + slot]))
        loads.append(pltpu.make_async_copy(v_hbm.at[:, head_cols(slot, HEAD_WIDTH)], v_in.at[slot], in_sem.at[5 + slot]))
    for slot in (1, 0):
        loads.append(pltpu.make_async_copy(q_hbm.at[:, head_cols(slot, COLS)], q_in.at[slot], in_sem.at[7 + slot]))
    for load in loads:
        load.start()

    for load in loads[:3]:
        load.wait()
    pos = pos_in[...].astype(jnp.float32)
    reset = reset_in[...].astype(jnp.float32)
    sine, cosine = sine_cosine(freq_in[...] * reset)
    sine_rows = jnp.concatenate([-sine, sine], axis=0).T
    cosine_rows = jnp.concatenate([cosine, cosine], axis=0).T
    place[...] = jnp.concatenate([pos, pos - reset, jnp.zeros((6, ROWS), jnp.float32)], axis=0)
    bounds[0] = place[...]
    sine_q, cosine_q = sine * SCALE, cosine * SCALE

    my_slot = y * 2 + z
    for load in loads[3:7]:
        load.wait()

    def keys_of(slot):
        raw = k_in[slot].astype(jnp.float32)
        return (raw * cosine_rows + pltpu.roll(raw, HALF, 1) * sine_rows).astype(jnp.bfloat16)

    def values_of(slot):
        return v_in[slot].astype(jnp.float32).T.astype(jnp.bfloat16)

    stage[0:ROWS] = keys_of(1)
    stage[ROWS : 2 * ROWS] = values_of(1)
    items[my_slot, 0:ROWS] = keys_of(0)
    items[my_slot, ROWS : 2 * ROWS] = values_of(0)

    pl.semaphore_wait(barrier, 4)

    to_sibling = [
        pltpu.make_async_remote_copy(
            src_ref=place, dst_ref=place_sib, send_sem=sib_sem.at[0], recv_sem=sib_sem.at[1],
            device_id=sibling, device_id_type=MESH,
        ),
        pltpu.make_async_remote_copy(
            src_ref=stage, dst_ref=items.at[my_slot, pl.ds(256, 256)], send_sem=sib_sem.at[2],
            recv_sem=sib_sem.at[3], device_id=sibling, device_id_type=MESH,
        ),
        pltpu.make_async_remote_copy(
            src_ref=q_stage, dst_ref=q_t.at[pl.ds(0, HEAD_WIDTH), pl.ds(COLS, COLS)], send_sem=sib_sem.at[4],
            recv_sem=sib_sem.at[5], device_id=sibling, device_id_type=MESH,
        ),
    ]

    def part_copy(sub, slot, target):
        rows = items.at[slot, pl.ds(*SUB_ROWS[sub])]
        return pltpu.make_async_remote_copy(
            src_ref=rows, dst_ref=rows, send_sem=send_sem, recv_sem=item_sem.at[sub, slot],
            device_id=target, device_id_type=MESH,
        )

    children = {}
    for sub, node, parent in PLAN["edges"]:
        children.setdefault((sub, parent), []).append(node)

    def slot_of(node):
        return around(y - node[0]) * 2 + (z if node[1] == 0 else 1 - z)

    def hand_on(sub, node):
        for child in children.get((sub, node), []):
            target = device(around(y + child[0] - node[0]), z if child[1] == node[1] else 1 - z, core)
            part_copy(sub, slot_of(node), target).start()

    def receive(sub, node):
        part_copy(sub, slot_of(node), sibling).wait_recv()
        hand_on(sub, node)

    def rotate_queries(slot):
        for head in range(GROUP):
            cols = slice(head * ROWS, (head + 1) * ROWS)
            raw = q_in[slot, :, cols].astype(jnp.float32).T
            low, high = raw[:HALF], raw[HALF:]
            turned = jnp.concatenate(
                [low * cosine_q - high * sine_q, high * cosine_q + low * sine_q], axis=0
            ).astype(jnp.bfloat16)
            if slot == 0:
                q_t[0:HEAD_WIDTH, cols] = turned
            else:
                q_stage[:, cols] = turned

    to_sibling[0].start()
    to_sibling[1].start()
    hand_on(0, (0, 0))

    loads[7].wait()
    rotate_queries(1)
    to_sibling[2].start()

    to_sibling[0].wait_recv()
    bounds[1] = place_sib[...]
    place_rows = []
    for group in range(2):
        at = bounds[group, 0:1]
        high = jnp.floor(at * (1.0 / 64.0))
        place_rows += [high, at - high * 64.0]
    items[my_slot, 512:528] = jnp.concatenate(
        place_rows + [jnp.zeros((12, ROWS), jnp.float32)], axis=0
    ).astype(jnp.bfloat16)
    to_sibling[1].wait_recv()
    hand_on(1, (0, 0))

    loads[8].wait()
    rotate_queries(0)
    unit_matrix = (
        lax.broadcasted_iota(jnp.int32, (ROWS, ROWS), 0) == lax.broadcasted_iota(jnp.int32, (ROWS, ROWS), 1)
    ).astype(jnp.float32).astype(jnp.bfloat16)
    for head in range(2 * GROUP):
        q_t[HEAD_WIDTH:, head * ROWS : (head + 1) * ROWS] = unit_matrix
    top[...] = jnp.full_like(top, MASKED)
    total[...] = jnp.zeros_like(total)
    acc[...] = jnp.zeros_like(acc)
    to_sibling[2].wait_recv()

    steps = PLAN["steps"]
    units = [(step, unit) for step in range(len(steps)) for unit in range(2 * COLS // UNIT)]

    def prepare(step):
        row = 0
        for node in steps[step]:
            slot = slot_of(node)
            tile = items[slot, 512:528].astype(jnp.float32)
            for part in range(2):
                at = tile[2 * part : 2 * part + 1] * 64.0 + tile[2 * part + 1 : 2 * part + 2]
                at = jnp.broadcast_to(at, (ROWS, ROWS)).T
                for group in range(2):
                    seen = (at <= bounds[group, 0:1]) & (at >= bounds[group, 1:2])
                    mask[step % 2, group, row : row + ROWS] = jnp.where(seen, 0.0, MASKED).astype(jnp.bfloat16)
                row += ROWS

    def score(step, unit):
        group = unit * UNIT // COLS
        keys = []
        for node in steps[step]:
            slot = slot_of(node)
            keys += [items[slot, 0:ROWS], items[slot, 256 : 256 + ROWS]]
        keys = jnp.concatenate(keys, axis=0)
        left = jnp.concatenate([keys, mask[step % 2, group, : keys.shape[0]]], axis=1)
        return jnp.dot(left, q_t[:, unit * UNIT : (unit + 1) * UNIT], preferred_element_type=jnp.float32)

    def weigh(unit, scores):
        cols = slice(unit * UNIT, (unit + 1) * UNIT)
        before = top[:, cols]
        now = jnp.maximum(before, jnp.max(scores, axis=0, keepdims=True))
        rescale = jnp.exp2(before - now)
        top[:, cols] = now
        weights = jnp.exp2(scores - now)
        total[:, cols] = total[:, cols] * rescale + jnp.sum(weights, axis=0, keepdims=True)
        return weights.astype(jnp.bfloat16), rescale

    def gather_values(step, unit, weights, rescale):
        cols = slice(unit * UNIT, (unit + 1) * UNIT)
        values = []
        for node in steps[step]:
            slot = slot_of(node)
            values += [items[slot, ROWS : 2 * ROWS], items[slot, 256 + ROWS : 512]]
        values = jnp.concatenate(values, axis=1)
        acc[:, cols] = acc[:, cols] * rescale + jnp.dot(values, weights, preferred_element_type=jnp.float32)

    def finish(group):
        for head in range(GROUP):
            cols = slice(group * COLS + head * ROWS, group * COLS + (head + 1) * ROWS)
            result = acc[:, cols] / total[:, cols]
            out_buf[group, :, head * ROWS : (head + 1) * ROWS] = result.T.astype(jnp.bfloat16)

    out_cols = pl.ds(pl.multiple_of(core * COLS, COLS), COLS)
    back = pltpu.make_async_remote_copy(
        src_ref=out_buf.at[1], dst_ref=out_hbm.at[:, out_cols], send_sem=out_sem.at[0], recv_sem=out_sem.at[1],
        device_id=sibling, device_id_type=MESH,
    )
    keep = pltpu.make_async_copy(out_buf.at[0], out_hbm.at[:, out_cols], out_sem.at[2])

    waits = PLAN["waits"]
    made = 0

    def make_waits(count):
        nonlocal made
        while made < count:
            receive(*waits[made])
            made += 1

    def scores_of(index):
        make_waits(PLAN["before"][index])
        step, unit = units[index]
        if unit == UNIT_ORDER[0]:
            prepare(step)
        return score(step, unit)

    units = [(step, unit) for step in range(len(steps)) for unit in UNIT_ORDER]
    coming = scores_of(0)
    pending = None
    for index, (step, unit) in enumerate(units):
        scores = coming
        if index + 1 < len(units):
            coming = scores_of(index + 1)
        weights, rescale = weigh(unit, scores)
        if pending is not None:
            gather_values(*pending)
        pending = (step, unit, weights, rescale)
        if index == len(units) - 2:
            pass
    gather_values(*pending)
    finish(1)
    back.start()
    finish(0)
    keep.start()

    all_parts = items.at[pl.ds(0, 2 * NY - 1)]
    pltpu.make_async_copy(all_parts, all_parts, send_sem).wait()
    for copy in to_sibling:
        copy.wait_send()
    back.wait()
    keep.wait()


UNIT_ORDER = tuple(range(2 * COLS // UNIT))[::-1]


def on_device(queries, keys, values, loader_pos, reset_pos, doc_starts):
    del doc_starts
    frequency = (ROPE_BASE ** (-np.arange(HALF, dtype=np.float64) * 2.0 / HEAD_WIDTH)).astype(np.float32)
    frequency = jnp.asarray(np.broadcast_to(frequency[:, None], (HALF, ROWS)))
    bf16, f32 = jnp.bfloat16, jnp.float32
    return pl.pallas_call(
        kernel,
        out_shape=jax.ShapeDtypeStruct((ROWS, 2 * COLS), bf16),
        in_specs=[pl.BlockSpec(memory_space=pl.ANY)] * 6,
        out_specs=pl.BlockSpec(memory_space=pl.ANY),
        scratch_shapes=[
            pltpu.VMEM((2, ROWS, COLS), bf16),
            pltpu.VMEM((2, ROWS, HEAD_WIDTH), bf16),
            pltpu.VMEM((2, ROWS, HEAD_WIDTH), bf16),
            pltpu.VMEM((1, ROWS), jnp.int32),
            pltpu.VMEM((1, ROWS), jnp.int32),
            pltpu.VMEM((HALF, ROWS), f32),
            pltpu.VMEM((2 * NY, ITEM_ROWS, HEAD_WIDTH), bf16),
            pltpu.VMEM((256, HEAD_WIDTH), bf16),
            pltpu.VMEM((2 * HEAD_WIDTH, 2 * COLS), bf16),
            pltpu.VMEM((HEAD_WIDTH, COLS), bf16),
            pltpu.VMEM((8, ROWS), f32),
            pltpu.VMEM((8, ROWS), f32),
            pltpu.VMEM((2, 8, ROWS), f32),
            pltpu.VMEM((2, 2, 4 * ROWS, ROWS), bf16),
            pltpu.VMEM((1, 2 * COLS), f32),
            pltpu.VMEM((1, 2 * COLS), f32),
            pltpu.VMEM((HEAD_WIDTH, 2 * COLS), f32),
            pltpu.VMEM((2, ROWS, COLS), bf16),
            pltpu.SemaphoreType.DMA((9,)),
            pltpu.SemaphoreType.DMA((2, 2 * NY)),
            pltpu.SemaphoreType.DMA((6,)),
            pltpu.SemaphoreType.DMA,
            pltpu.SemaphoreType.DMA((3,)),
        ],
        compiler_params=pltpu.CompilerParams(
            collective_id=0, has_side_effects=True, vmem_limit_bytes=48 * 2**20
        ),
    )(queries, keys, values, loader_pos.reshape(1, ROWS), reset_pos.reshape(1, ROWS), frequency)


def solution(mesh):
    rows = ("dp", "ctx")
    return jax.shard_map(
        on_device,
        mesh=mesh,
        in_specs=(P(rows, "tp"), P(rows, "tp"), P(rows, "tp"), P(rows), P(rows), P("dp")),
        out_specs=P(rows, "tp"),
        check_vma=False,
    )
```

```python
import functools
import math

import jax
import jax.numpy as jnp
import numpy as np
from jax import lax
from jax.experimental import pallas as pl
from jax.experimental.pallas import tpu as pltpu
from jax.sharding import PartitionSpec as P

MESH = pl.DeviceIdType.MESH
HEAD_WIDTH = 128
HALF = HEAD_WIDTH // 2
ROPE_BASE = 1000000.0
SCALE = math.log2(math.e) / math.sqrt(HEAD_WIDTH)
ROWS = 128
GROUP = 8
COLS = GROUP * ROWS
NY = 8
UNIT = 512
MASKED = -1e30
ITEM_ROWS = 528

PLAN = {
    "parts": [
        (0, 128), (128, 128), (256, 128), (384, 144),
    ],
    "edges": [
        (0, (-3, 0), (-2, 0)), (0, (-3, 1), (-2, 1)), (0, (-2, 0), (-1, 0)), (0, (-2, 1), (-1, 1)),
        (0, (-1, 0), (0, 0)), (0, (-1, 1), (-1, 0)), (0, (0, 1), (0, 0)), (0, (1, 0), (0, 0)), (0, (1, 1), (0, 1)),
        (0, (2, 0), (1, 0)), (0, (2, 1), (1, 1)), (0, (3, 0), (2, 0)), (0, (3, 1), (2, 1)), (0, (4, 0), (-3, 0)),
        (0, (4, 1), (-3, 1)), (1, (-3, 0), (-2, 0)), (1, (-3, 1), (-3, 0)), (1, (-2, 0), (-1, 0)),
        (1, (-2, 1), (-2, 0)), (1, (-1, 0), (0, 0)), (1, (-1, 1), (-1, 0)), (1, (0, 1), (0, 0)),
        (1, (1, 0), (0, 0)), (1, (1, 1), (0, 1)), (1, (2, 0), (1, 0)), (1, (2, 1), (1, 1)), (1, (3, 0), (2, 0)),
        (1, (3, 1), (2, 1)), (1, (4, 0), (-3, 0)), (1, (4, 1), (-3, 1)), (2, (-3, 0), (-2, 0)),
        (2, (-3, 1), (-3, 0)), (2, (-2, 0), (-1, 0)), (2, (-2, 1), (-2, 0)), (2, (-1, 0), (0, 0)),
        (2, (-1, 1), (-1, 0)), (2, (0, 1), (0, 0)), (2, (1, 0), (0, 0)), (2, (1, 1), (1, 0)), (2, (2, 0), (1, 0)),
        (2, (2, 1), (1, 1)), (2, (3, 0), (2, 0)), (2, (3, 1), (2, 1)), (2, (4, 0), (-3, 0)), (2, (4, 1), (4, 0)),
        (3, (-3, 0), (-2, 0)), (3, (-3, 1), (-2, 1)), (3, (-2, 0), (-1, 0)), (3, (-2, 1), (-2, 0)),
        (3, (-1, 0), (0, 0)), (3, (-1, 1), (0, 1)), (3, (0, 1), (0, 0)), (3, (1, 0), (0, 0)), (3, (1, 1), (1, 0)),
        (3, (2, 0), (1, 0)), (3, (2, 1), (2, 0)), (3, (3, 0), (2, 0)), (3, (3, 1), (3, 0)), (3, (4, 0), (-3, 0)),
        (3, (4, 1), (-3, 1)),
    ],
    "waits": [
        (0, (0, 1)), (0, (-1, 0)), (1, (0, 1)), (1, (-1, 0)), (0, (1, 0)), (2, (0, 1)), (2, (-1, 0)), (3, (0, 1)),
        (1, (1, 0)), (2, (1, 0)), (3, (-1, 0)), (0, (-1, 1)), (3, (1, 0)), (0, (1, 1)), (1, (-1, 1)), (1, (-2, 0)),
        (0, (-2, 0)), (2, (-1, 1)), (1, (1, 1)), (2, (-2, 0)), (0, (2, 0)), (2, (1, 1)), (3, (-1, 1)), (3, (-2, 0)),
        (1, (2, 0)), (3, (1, 1)), (0, (-2, 1)), (2, (2, 0)), (3, (2, 0)), (1, (-3, 0)), (0, (-3, 0)), (1, (-2, 1)),
        (0, (2, 1)), (3, (-2, 1)), (2, (-2, 1)), (2, (-3, 0)), (3, (-3, 0)), (0, (3, 0)), (1, (2, 1)), (2, (2, 1)),
        (3, (2, 1)), (1, (4, 0)), (1, (-3, 1)), (1, (3, 0)), (2, (3, 0)), (0, (-3, 1)), (3, (3, 0)), (0, (4, 0)),
        (3, (-3, 1)), (2, (-3, 1)), (2, (4, 0)), (0, (3, 1)), (3, (4, 0)), (1, (3, 1)), (1, (4, 1)), (2, (3, 1)),
        (3, (3, 1)), (2, (4, 1)), (3, (4, 1)), (0, (4, 1)),
    ],
    "steps": [
        [(0, 0)], [(0, 1), (-1, 0)], [(1, 0), (-1, 1)], [(-2, 0), (1, 1)], [(2, 0), (-2, 1)], [(-3, 0), (2, 1)],
        [(3, 0), (-3, 1)], [(4, 0), (3, 1)], [(4, 1)],
    ],
    "before": [
        0, 0, 0, 0, 11, 11, 13, 17, 23, 23, 25, 26, 29, 30, 33, 35, 36, 36, 36, 37, 45, 45, 48, 50, 51, 51, 52, 53,
        57, 57, 57, 57, 60, 60, 60, 60,
    ],
}


def sine_cosine(angle):
    turn = jnp.floor(angle * (2.0 / math.pi) + 0.5)
    rest = ((angle - turn * 1.5703125) - turn * 4.837512969970703125e-4) - turn * 7.54978995489188216e-8
    square = rest * rest
    sine = ((-1.9515295891e-4 * square + 8.3321608736e-3) * square - 1.6666654611e-1) * square * rest + rest
    cosine = (
        (2.443315711809948e-5 * square - 1.388731625493765e-3) * square + 4.166664568298827e-2
    ) * square * square - 0.5 * square + 1.0
    quarter = turn.astype(jnp.int32)
    swap = (quarter & 1) == 1
    sine_out = jnp.where(swap, cosine, sine)
    cosine_out = jnp.where(swap, sine, cosine)
    sine_out = jnp.where((quarter & 2) == 2, -sine_out, sine_out)
    cosine_out = jnp.where(((quarter + 1) & 2) == 2, -cosine_out, cosine_out)
    return sine_out, cosine_out


def frequencies():
    row = lax.broadcasted_iota(jnp.int32, (8, ROWS), 0)
    tiles = []
    for first in range(0, HALF, 8):
        tile = jnp.zeros((8, ROWS), jnp.float32)
        for i in range(8):
            tile = jnp.where(row == i, float(np.float32(ROPE_BASE ** (-2.0 * (first + i) / HEAD_WIDTH))), tile)
        tiles.append(tile)
    return jnp.concatenate(tiles, axis=0)


def kernel(
    q_hbm, k_hbm, v_hbm, pos_hbm, reset_hbm, out_ref,
    q_in, k_in, v_in, pos_in, reset_in,
    items, stage, q_t, q_stage, place, place_sib, bounds, mask, top, total, acc, out_buf,
    in_sem, item_sem, sib_sem, send_sem, out_sem,
):
    ctx = lax.axis_index("ctx")
    tp = lax.axis_index("tp")
    dp = lax.axis_index("dp")
    y, z, core = ctx // 4, (ctx // 2) % 2, ctx % 2

    def device(yy, zz, cc):
        return ((yy * 2 + zz) * 2 + cc, tp, dp)

    def around(yy):
        return lax.rem(yy + 2 * NY, NY)

    sibling = device(y, z, 1 - core)

    barrier = pltpu.get_barrier_semaphore()
    strides = set()
    for _, node, parent in PLAN["edges"]:
        stride = ((node[0] - parent[0]) % NY, node[1] ^ parent[1])
        strides |= {stride, (-stride[0] % NY, stride[1])}
    partners = [device(around(y + dy), z if dz == 0 else 1 - z, core) for dy, dz in sorted(strides)] + [sibling]
    for other in partners:
        pl.semaphore_signal(barrier, inc=1, device_id=other, device_id_type=MESH)

    def head_cols(slot, width):
        head = core if slot == 0 else 1 - core
        return pl.ds(pl.multiple_of(head * width, width), width)

    loads = [
        pltpu.make_async_copy(pos_hbm, pos_in, in_sem.at[0]),
        pltpu.make_async_copy(reset_hbm, reset_in, in_sem.at[1]),
    ]
    for slot in (1, 0):
        loads.append(pltpu.make_async_copy(k_hbm.at[:, head_cols(slot, HEAD_WIDTH)], k_in.at[slot], in_sem.at[2 + slot]))
        loads.append(pltpu.make_async_copy(v_hbm.at[:, head_cols(slot, HEAD_WIDTH)], v_in.at[slot], in_sem.at[4 + slot]))
    for slot in (1, 0):
        loads.append(pltpu.make_async_copy(q_hbm.at[:, head_cols(slot, COLS)], q_in.at[slot], in_sem.at[6 + slot]))
    for load in loads:
        load.start()

    for load in loads[:2]:
        load.wait()
    pos = pos_in[...].reshape(1, ROWS).astype(jnp.float32)
    reset = reset_in[...].reshape(1, ROWS).astype(jnp.float32)
    sine, cosine = sine_cosine(frequencies() * reset)
    sine_rows = jnp.concatenate([-sine, sine], axis=0).T
    cosine_rows = jnp.concatenate([cosine, cosine], axis=0).T
    place[...] = jnp.concatenate([pos, pos - reset, jnp.zeros((6, ROWS), jnp.float32)], axis=0)
    bounds[0] = place[...]
    sine_q, cosine_q = sine * SCALE, cosine * SCALE

    my_slot = y * 2 + z
    for load in loads[2:6]:
        load.wait()

    def keys_of(slot):
        raw = k_in[slot].astype(jnp.float32)
        return (raw * cosine_rows + pltpu.roll(raw, HALF, 1) * sine_rows).astype(jnp.bfloat16)

    def values_of(slot):
        return v_in[slot].astype(jnp.float32).T.astype(jnp.bfloat16)

    stage[0:ROWS] = keys_of(1)
    stage[ROWS : 2 * ROWS] = values_of(1)
    items[my_slot, 0:ROWS] = keys_of(0)
    items[my_slot, ROWS : 2 * ROWS] = values_of(0)

    pl.semaphore_wait(barrier, len(partners))

    to_sibling = [
        pltpu.make_async_remote_copy(
            src_ref=place, dst_ref=place_sib, send_sem=sib_sem.at[0], recv_sem=sib_sem.at[1],
            device_id=sibling, device_id_type=MESH,
        ),
        pltpu.make_async_remote_copy(
            src_ref=stage, dst_ref=items.at[my_slot, pl.ds(256, 256)], send_sem=sib_sem.at[2],
            recv_sem=sib_sem.at[3], device_id=sibling, device_id_type=MESH,
        ),
        pltpu.make_async_remote_copy(
            src_ref=q_stage, dst_ref=q_t.at[pl.ds(0, HEAD_WIDTH), pl.ds(COLS, COLS)], send_sem=sib_sem.at[4],
            recv_sem=sib_sem.at[5], device_id=sibling, device_id_type=MESH,
        ),
    ]

    def part_copy(sub, slot, target):
        rows = items.at[slot, pl.ds(*PLAN["parts"][sub])]
        return pltpu.make_async_remote_copy(
            src_ref=rows, dst_ref=rows, send_sem=send_sem, recv_sem=item_sem.at[sub, slot],
            device_id=target, device_id_type=MESH,
        )

    children = {}
    for sub, node, parent in PLAN["edges"]:
        children.setdefault((sub, parent), []).append(node)

    def slot_of(node):
        return around(y - node[0]) * 2 + (z if node[1] == 0 else 1 - z)

    def hand_on(sub, node):
        for child in children.get((sub, node), []):
            target = device(around(y + child[0] - node[0]), z if child[1] == node[1] else 1 - z, core)
            part_copy(sub, slot_of(node), target).start()

    def receive(sub, node):
        part_copy(sub, slot_of(node), sibling).wait_recv()
        hand_on(sub, node)

    def rotate_queries(slot):
        for head in range(GROUP):
            cols = slice(head * ROWS, (head + 1) * ROWS)
            raw = q_in[slot, :, cols].astype(jnp.float32).T
            low, high = raw[:HALF], raw[HALF:]
            turned = jnp.concatenate(
                [low * cosine_q - high * sine_q, high * cosine_q + low * sine_q], axis=0
            ).astype(jnp.bfloat16)
            if slot == 0:
                q_t[0:HEAD_WIDTH, cols] = turned
            else:
                q_stage[:, cols] = turned

    to_sibling[0].start()
    to_sibling[1].start()
    for part, (first, _) in enumerate(PLAN["parts"]):
        if first < 256:
            hand_on(part, (0, 0))
    loads[7].wait()
    rotate_queries(0)

    to_sibling[0].wait_recv()
    bounds[1] = place_sib[...]
    place_rows = []
    for group in range(2):
        at = bounds[group, 0:1]
        high = jnp.floor(at * (1.0 / 64.0))
        place_rows += [high, at - high * 64.0]
    items[my_slot, 512:528] = jnp.concatenate(
        place_rows + [jnp.zeros((12, ROWS), jnp.float32)], axis=0
    ).astype(jnp.bfloat16)
    to_sibling[1].wait_recv()
    for part, (first, _) in enumerate(PLAN["parts"]):
        if first >= 256:
            hand_on(part, (0, 0))

    loads[6].wait()
    rotate_queries(1)
    to_sibling[2].start()
    unit_matrix = (
        lax.broadcasted_iota(jnp.int32, (ROWS, ROWS), 0) == lax.broadcasted_iota(jnp.int32, (ROWS, ROWS), 1)
    ).astype(jnp.float32).astype(jnp.bfloat16)
    for head in range(2 * GROUP):
        q_t[HEAD_WIDTH:, head * ROWS : (head + 1) * ROWS] = unit_matrix
    top[...] = jnp.full_like(top, MASKED)
    total[...] = jnp.zeros_like(total)
    acc[...] = jnp.zeros_like(acc)

    steps = PLAN["steps"]
    per_step = 2 * COLS // UNIT
    units = [(0, unit) for unit in range(per_step)]
    units += [(step, unit) for step in range(1, len(steps)) for unit in reversed(range(per_step))]

    def prepare(step):
        row = 0
        for node in steps[step]:
            slot = slot_of(node)
            tile = items[slot, 512:528].astype(jnp.float32)
            for part in range(2):
                at = tile[2 * part : 2 * part + 1] * 64.0 + tile[2 * part + 1 : 2 * part + 2]
                at = jnp.broadcast_to(at, (ROWS, ROWS)).T
                for group in range(2):
                    seen = (at <= bounds[group, 0:1]) & (at >= bounds[group, 1:2])
                    mask[step % 2, group, row : row + ROWS] = jnp.where(seen, 0.0, MASKED).astype(jnp.bfloat16)
                row += ROWS

    def score(step, unit):
        group = unit * UNIT // COLS
        keys = []
        for node in steps[step]:
            slot = slot_of(node)
            keys += [items[slot, 0:ROWS], items[slot, 256 : 256 + ROWS]]
        keys = jnp.concatenate(keys, axis=0)
        left = jnp.concatenate([keys, mask[step % 2, group, : keys.shape[0]]], axis=1)
        return jnp.dot(left, q_t[:, unit * UNIT : (unit + 1) * UNIT], preferred_element_type=jnp.float32)

    def weigh(unit, scores):
        cols = slice(unit * UNIT, (unit + 1) * UNIT)
        before = top[:, cols]
        now = jnp.maximum(before, jnp.max(scores, axis=0, keepdims=True))
        rescale = jnp.exp2(before - now)
        top[:, cols] = now
        weights = jnp.exp2(scores - now)
        total[:, cols] = total[:, cols] * rescale + jnp.sum(weights, axis=0, keepdims=True)
        return weights.astype(jnp.bfloat16), rescale

    def gather_values(step, unit, weights, rescale):
        cols = slice(unit * UNIT, (unit + 1) * UNIT)
        values = []
        for node in steps[step]:
            slot = slot_of(node)
            values += [items[slot, ROWS : 2 * ROWS], items[slot, 256 + ROWS : 512]]
        values = jnp.concatenate(values, axis=1)
        acc[:, cols] = acc[:, cols] * rescale + jnp.dot(values, weights, preferred_element_type=jnp.float32)

    def finish(group):
        for head in range(GROUP):
            cols = slice(group * COLS + head * ROWS, group * COLS + (head + 1) * ROWS)
            result = (acc[:, cols] / total[:, cols]).T.astype(jnp.bfloat16)
            if group == 0:
                out_ref[:, pl.ds(pl.multiple_of(core * COLS + head * ROWS, ROWS), ROWS)] = result
            else:
                out_buf[:, head * ROWS : (head + 1) * ROWS] = result

    back = pltpu.make_async_remote_copy(
        src_ref=out_buf, dst_ref=out_ref.at[:, pl.ds(pl.multiple_of(core * COLS, COLS), COLS)],
        send_sem=out_sem.at[0], recv_sem=out_sem.at[1], device_id=sibling, device_id_type=MESH,
    )

    waits = PLAN["waits"]
    made = 0

    def make_waits(count):
        nonlocal made
        while made < count:
            receive(*waits[made])
            made += 1

    def scores_of(index):
        make_waits(PLAN["before"][index])
        step, unit = units[index]
        if index % per_step == 0:
            prepare(step)
        if index == per_step // 2:
            to_sibling[2].wait_recv()
        return score(step, unit)

    coming = scores_of(0)
    pending = None
    for index, (step, unit) in enumerate(units):
        scores = coming
        if index + 1 < len(units):
            coming = scores_of(index + 1)
        weights, rescale = weigh(unit, scores)
        if pending is not None:
            gather_values(*pending)
        pending = (step, unit, weights, rescale)
        if index == len(units) - per_step // 2:
            finish(1)
            back.start()
    gather_values(*pending)
    finish(0)

    all_parts = items.at[pl.ds(0, 2 * NY - 1)]
    pltpu.make_async_copy(all_parts, all_parts, send_sem).wait()
    for copy in to_sibling:
        copy.wait_send()
    back.wait()


def on_device(queries, keys, values, loader_pos, reset_pos, doc_starts):
    del doc_starts
    bf16, f32 = jnp.bfloat16, jnp.float32
    return pl.pallas_call(
        kernel,
        out_shape=pltpu.VMEM((ROWS, 2 * COLS), bf16),
        in_specs=[pl.BlockSpec(memory_space=pltpu.HBM)] * 5,
        out_specs=pl.BlockSpec(memory_space=pltpu.VMEM),
        scratch_shapes=[
            pltpu.VMEM((2, ROWS, COLS), bf16),
            pltpu.VMEM((2, ROWS, HEAD_WIDTH), bf16),
            pltpu.VMEM((2, ROWS, HEAD_WIDTH), bf16),
            pltpu.VMEM((ROWS,), jnp.int32),
            pltpu.VMEM((ROWS,), jnp.int32),
            pltpu.VMEM((2 * NY, ITEM_ROWS, HEAD_WIDTH), bf16),
            pltpu.VMEM((256, HEAD_WIDTH), bf16),
            pltpu.VMEM((2 * HEAD_WIDTH, 2 * COLS), bf16),
            pltpu.VMEM((HEAD_WIDTH, COLS), bf16),
            pltpu.VMEM((8, ROWS), f32),
            pltpu.VMEM((8, ROWS), f32),
            pltpu.VMEM((2, 8, ROWS), f32),
            pltpu.VMEM((2, 2, 4 * ROWS, ROWS), bf16),
            pltpu.VMEM((1, 2 * COLS), f32),
            pltpu.VMEM((1, 2 * COLS), f32),
            pltpu.VMEM((HEAD_WIDTH, 2 * COLS), f32),
            pltpu.VMEM((ROWS, COLS), bf16),
            pltpu.SemaphoreType.DMA((8,)),
            pltpu.SemaphoreType.DMA((len(PLAN["parts"]), 2 * NY)),
            pltpu.SemaphoreType.DMA((6,)),
            pltpu.SemaphoreType.DMA,
            pltpu.SemaphoreType.DMA((2,)),
        ],
        compiler_params=pltpu.CompilerParams(
            collective_id=0, has_side_effects=True, vmem_limit_bytes=60 * 2**20
        ),
    )(*(pltpu.with_memory_space_constraint(x, pltpu.HBM) for x in (queries, keys, values, loader_pos, reset_pos)))


def solution(mesh):
    rows = ("dp", "ctx")
    return jax.shard_map(
        on_device,
        mesh=mesh,
        in_specs=(P(rows, "tp"), P(rows, "tp"), P(rows, "tp"), P(rows), P(rows), P("dp")),
        out_specs=P(rows, "tp"),
        check_vma=False,
    )
```

```python
import functools
import math

import jax
import jax.numpy as jnp
import numpy as np
from jax import lax
from jax.experimental import pallas as pl
from jax.experimental.pallas import tpu as pltpu
from jax.sharding import PartitionSpec as P

MESH = pl.DeviceIdType.MESH
HEAD_WIDTH = 128
HALF = HEAD_WIDTH // 2
ROPE_BASE = 1000000.0
SCALE = math.log2(math.e) / math.sqrt(HEAD_WIDTH)
ROWS = 128
GROUP = 8
COLS = GROUP * ROWS
NY = 8
UNIT = 512
MASKED = -1e30
ITEM_ROWS = 528

PLAN = {
    "parts": [
        (0, 256), (256, 272),
    ],
    "edges": [
        (0, (-3, 0), (-2, 0)), (0, (-3, 1), (-3, 0)), (0, (-2, 0), (-1, 0)), (0, (-2, 1), (-2, 0)),
        (0, (-1, 0), (0, 0)), (0, (-1, 1), (-1, 0)), (0, (0, 1), (0, 0)), (0, (1, 0), (0, 0)), (0, (1, 1), (1, 0)),
        (0, (2, 0), (1, 0)), (0, (2, 1), (1, 1)), (0, (3, 0), (2, 0)), (0, (3, 1), (3, 0)), (0, (4, 0), (-3, 0)),
        (0, (4, 1), (-3, 1)), (1, (-3, 0), (-2, 0)), (1, (-3, 1), (-3, 0)), (1, (-2, 0), (-1, 0)),
        (1, (-2, 1), (-1, 1)), (1, (-1, 0), (0, 0)), (1, (-1, 1), (-1, 0)), (1, (0, 1), (0, 0)),
        (1, (1, 0), (0, 0)), (1, (1, 1), (0, 1)), (1, (2, 0), (1, 0)), (1, (2, 1), (2, 0)), (1, (3, 0), (2, 0)),
        (1, (3, 1), (2, 1)), (1, (4, 0), (-3, 0)), (1, (4, 1), (4, 0)),
    ],
    "waits": [
        (0, (-1, 0)), (0, (1, 0)), (0, (0, 1)), (1, (-1, 0)), (1, (1, 0)), (1, (0, 1)), (0, (-2, 0)), (0, (-1, 1)),
        (1, (-2, 0)), (0, (1, 1)), (0, (2, 0)), (1, (-1, 1)), (1, (2, 0)), (0, (-3, 0)), (1, (-3, 0)), (1, (1, 1)),
        (0, (-2, 1)), (1, (2, 1)), (0, (2, 1)), (0, (3, 0)), (1, (-2, 1)), (0, (-3, 1)), (0, (4, 0)), (1, (4, 0)),
        (1, (-3, 1)), (1, (3, 0)), (1, (3, 1)), (0, (3, 1)), (0, (4, 1)), (1, (4, 1)),
    ],
    "steps": [
        [(0, 0)], [(-1, 0), (1, 0)], [(0, 1), (-2, 0)], [(-1, 1), (2, 0)], [(-3, 0), (1, 1)], [(2, 1), (-2, 1)],
        [(4, 0), (-3, 1)], [(3, 0), (3, 1)], [(4, 1)],
    ],
    "before": [
        0, 0, 0, 0, 5, 7, 7, 7, 10, 10, 14, 14, 14, 14, 15, 17, 17, 17, 18, 19, 22, 22, 22, 25, 26, 26, 26, 26, 28,
        28, 28, 28, 30, 30, 30, 30,
    ],
}


def sine_cosine(angle):
    turn = jnp.floor(angle * (2.0 / math.pi) + 0.5)
    rest = ((angle - turn * 1.5703125) - turn * 4.837512969970703125e-4) - turn * 7.54978995489188216e-8
    square = rest * rest
    sine = ((-1.9515295891e-4 * square + 8.3321608736e-3) * square - 1.6666654611e-1) * square * rest + rest
    cosine = (
        (2.443315711809948e-5 * square - 1.388731625493765e-3) * square + 4.166664568298827e-2
    ) * square * square - 0.5 * square + 1.0
    quarter = turn.astype(jnp.int32)
    swap = (quarter & 1) == 1
    sine_out = jnp.where(swap, cosine, sine)
    cosine_out = jnp.where(swap, sine, cosine)
    sine_out = jnp.where((quarter & 2) == 2, -sine_out, sine_out)
    cosine_out = jnp.where(((quarter + 1) & 2) == 2, -cosine_out, cosine_out)
    return sine_out, cosine_out


def frequencies():
    row = lax.broadcasted_iota(jnp.int32, (8, ROWS), 0)
    tiles = []
    for first in range(0, HALF, 8):
        tile = jnp.zeros((8, ROWS), jnp.float32)
        for i in range(8):
            tile = jnp.where(row == i, float(np.float32(ROPE_BASE ** (-2.0 * (first + i) / HEAD_WIDTH))), tile)
        tiles.append(tile)
    return jnp.concatenate(tiles, axis=0)


def kernel(
    q_hbm, k_hbm, v_hbm, pos_hbm, reset_hbm, out_ref,
    q_in, k_in, v_in, pos_in, reset_in,
    items, stage, q_t, q_stage, place, place_sib, bounds, mask, top, total, acc, out_buf,
    in_sem, item_sem, sib_sem, send_sem, out_sem,
):
    ctx = lax.axis_index("ctx")
    tp = lax.axis_index("tp")
    dp = lax.axis_index("dp")
    y, z, core = ctx // 4, (ctx // 2) % 2, ctx % 2

    def device(yy, zz, cc):
        return ((yy * 2 + zz) * 2 + cc, tp, dp)

    def around(yy):
        return lax.rem(yy + 2 * NY, NY)

    sibling = device(y, z, 1 - core)

    barrier = pltpu.get_barrier_semaphore()
    strides = set()
    for _, node, parent in PLAN["edges"]:
        stride = ((node[0] - parent[0]) % NY, node[1] ^ parent[1])
        strides |= {stride, (-stride[0] % NY, stride[1])}
    partners = [device(around(y + dy), z if dz == 0 else 1 - z, core) for dy, dz in sorted(strides)] + [sibling]
    for other in partners:
        pl.semaphore_signal(barrier, inc=1, device_id=other, device_id_type=MESH)

    def head_cols(slot, width):
        head = core if slot == 0 else 1 - core
        return pl.ds(pl.multiple_of(head * width, width), width)

    loads = [
        pltpu.make_async_copy(pos_hbm, pos_in, in_sem.at[0]),
        pltpu.make_async_copy(reset_hbm, reset_in, in_sem.at[1]),
    ]
    for slot in (1, 0):
        loads.append(pltpu.make_async_copy(k_hbm.at[:, head_cols(slot, HEAD_WIDTH)], k_in.at[slot], in_sem.at[2 + slot]))
        loads.append(pltpu.make_async_copy(v_hbm.at[:, head_cols(slot, HEAD_WIDTH)], v_in.at[slot], in_sem.at[4 + slot]))
    for slot in (1, 0):
        loads.append(pltpu.make_async_copy(q_hbm.at[:, head_cols(slot, COLS)], q_in.at[slot], in_sem.at[6 + slot]))
    for load in loads:
        load.start()

    for load in loads[:2]:
        load.wait()
    pos = pos_in[...].reshape(1, ROWS).astype(jnp.float32)
    reset = reset_in[...].reshape(1, ROWS).astype(jnp.float32)
    sine, cosine = sine_cosine(frequencies() * reset)
    sine_rows = jnp.concatenate([-sine, sine], axis=0).T
    cosine_rows = jnp.concatenate([cosine, cosine], axis=0).T
    place[...] = jnp.concatenate([pos, pos - reset, jnp.zeros((6, ROWS), jnp.float32)], axis=0)
    bounds[0] = place[...]
    sine_q, cosine_q = sine * SCALE, cosine * SCALE

    my_slot = y * 2 + z
    for load in loads[2:6]:
        load.wait()

    def keys_of(slot):
        raw = k_in[slot].astype(jnp.float32)
        return (raw * cosine_rows + pltpu.roll(raw, HALF, 1) * sine_rows).astype(jnp.bfloat16)

    def values_of(slot):
        return v_in[slot].astype(jnp.float32).T.astype(jnp.bfloat16)

    stage[0:ROWS] = keys_of(1)
    stage[ROWS : 2 * ROWS] = values_of(1)
    items[my_slot, 0:ROWS] = keys_of(0)
    items[my_slot, ROWS : 2 * ROWS] = values_of(0)

    pl.semaphore_wait(barrier, len(partners))

    to_sibling = [
        pltpu.make_async_remote_copy(
            src_ref=place, dst_ref=place_sib, send_sem=sib_sem.at[0], recv_sem=sib_sem.at[1],
            device_id=sibling, device_id_type=MESH,
        ),
        pltpu.make_async_remote_copy(
            src_ref=stage, dst_ref=items.at[my_slot, pl.ds(256, 256)], send_sem=sib_sem.at[2],
            recv_sem=sib_sem.at[3], device_id=sibling, device_id_type=MESH,
        ),
        pltpu.make_async_remote_copy(
            src_ref=q_stage, dst_ref=q_t.at[pl.ds(0, HEAD_WIDTH), pl.ds(COLS, COLS)], send_sem=sib_sem.at[4],
            recv_sem=sib_sem.at[5], device_id=sibling, device_id_type=MESH,
        ),
    ]

    def part_copy(sub, slot, target):
        rows = items.at[slot, pl.ds(*PLAN["parts"][sub])]
        return pltpu.make_async_remote_copy(
            src_ref=rows, dst_ref=rows, send_sem=send_sem, recv_sem=item_sem.at[sub, slot],
            device_id=target, device_id_type=MESH,
        )

    children = {}
    for sub, node, parent in PLAN["edges"]:
        children.setdefault((sub, parent), []).append(node)

    def slot_of(node):
        return around(y - node[0]) * 2 + (z if node[1] == 0 else 1 - z)

    def hand_on(sub, node):
        for child in children.get((sub, node), []):
            target = device(around(y + child[0] - node[0]), z if child[1] == node[1] else 1 - z, core)
            part_copy(sub, slot_of(node), target).start()

    def receive(sub, node):
        part_copy(sub, slot_of(node), sibling).wait_recv()
        hand_on(sub, node)

    def rotate_queries(slot):
        for head in range(GROUP):
            cols = slice(head * ROWS, (head + 1) * ROWS)
            raw = q_in[slot, :, cols].astype(jnp.float32).T
            low, high = raw[:HALF], raw[HALF:]
            turned = jnp.concatenate(
                [low * cosine_q - high * sine_q, high * cosine_q + low * sine_q], axis=0
            ).astype(jnp.bfloat16)
            if slot == 0:
                q_t[0:HEAD_WIDTH, cols] = turned
            else:
                q_stage[:, cols] = turned

    to_sibling[0].start()
    to_sibling[1].start()
    for part, (first, _) in enumerate(PLAN["parts"]):
        if first < 256:
            hand_on(part, (0, 0))
    loads[7].wait()
    rotate_queries(0)

    to_sibling[0].wait_recv()
    bounds[1] = place_sib[...]
    place_rows = []
    for group in range(2):
        at = bounds[group, 0:1]
        high = jnp.floor(at * (1.0 / 64.0))
        place_rows += [high, at - high * 64.0]
    items[my_slot, 512:528] = jnp.concatenate(
        place_rows + [jnp.zeros((12, ROWS), jnp.float32)], axis=0
    ).astype(jnp.bfloat16)
    to_sibling[1].wait_recv()
    for part, (first, _) in enumerate(PLAN["parts"]):
        if first >= 256:
            hand_on(part, (0, 0))

    loads[6].wait()
    rotate_queries(1)
    to_sibling[2].start()
    unit_matrix = (
        lax.broadcasted_iota(jnp.int32, (ROWS, ROWS), 0) == lax.broadcasted_iota(jnp.int32, (ROWS, ROWS), 1)
    ).astype(jnp.float32).astype(jnp.bfloat16)
    for head in range(2 * GROUP):
        q_t[HEAD_WIDTH:, head * ROWS : (head + 1) * ROWS] = unit_matrix
    top[...] = jnp.full_like(top, MASKED)
    total[...] = jnp.zeros_like(total)
    acc[...] = jnp.zeros_like(acc)

    steps = PLAN["steps"]
    per_step = 2 * COLS // UNIT
    units = [(0, unit) for unit in range(per_step)]
    units += [(step, unit) for step in range(1, len(steps)) for unit in reversed(range(per_step))]

    def prepare(step):
        row = 0
        for node in steps[step]:
            slot = slot_of(node)
            tile = items[slot, 512:528].astype(jnp.float32)
            for part in range(2):
                at = tile[2 * part : 2 * part + 1] * 64.0 + tile[2 * part + 1 : 2 * part + 2]
                at = jnp.broadcast_to(at, (ROWS, ROWS)).T
                for group in range(2):
                    seen = (at <= bounds[group, 0:1]) & (at >= bounds[group, 1:2])
                    mask[step % 2, group, row : row + ROWS] = jnp.where(seen, 0.0, MASKED).astype(jnp.bfloat16)
                row += ROWS

    def score(step, unit):
        group = unit * UNIT // COLS
        keys = []
        for node in steps[step]:
            slot = slot_of(node)
            keys += [items[slot, 0:ROWS], items[slot, 256 : 256 + ROWS]]
        keys = jnp.concatenate(keys, axis=0)
        left = jnp.concatenate([keys, mask[step % 2, group, : keys.shape[0]]], axis=1)
        return jnp.dot(left, q_t[:, unit * UNIT : (unit + 1) * UNIT], preferred_element_type=jnp.float32)

    def weigh(unit, scores):
        cols = slice(unit * UNIT, (unit + 1) * UNIT)
        before = top[:, cols]
        now = jnp.maximum(before, jnp.max(scores, axis=0, keepdims=True))
        rescale = jnp.exp2(before - now)
        top[:, cols] = now
        weights = jnp.exp2(scores - now)
        total[:, cols] = total[:, cols] * rescale + jnp.sum(weights, axis=0, keepdims=True)
        return weights.astype(jnp.bfloat16), rescale

    def gather_values(step, unit, weights, rescale):
        cols = slice(unit * UNIT, (unit + 1) * UNIT)
        values = []
        for node in steps[step]:
            slot = slot_of(node)
            values += [items[slot, ROWS : 2 * ROWS], items[slot, 256 + ROWS : 512]]
        values = jnp.concatenate(values, axis=1)
        acc[:, cols] = acc[:, cols] * rescale + jnp.dot(values, weights, preferred_element_type=jnp.float32)

    def finish(group):
        for head in range(GROUP):
            cols = slice(group * COLS + head * ROWS, group * COLS + (head + 1) * ROWS)
            result = (acc[:, cols] / total[:, cols]).T.astype(jnp.bfloat16)
            if group == 0:
                out_ref[:, pl.ds(pl.multiple_of(core * COLS + head * ROWS, ROWS), ROWS)] = result
            else:
                out_buf[:, head * ROWS : (head + 1) * ROWS] = result

    back = pltpu.make_async_remote_copy(
        src_ref=out_buf, dst_ref=out_ref.at[:, pl.ds(pl.multiple_of(core * COLS, COLS), COLS)],
        send_sem=out_sem.at[0], recv_sem=out_sem.at[1], device_id=sibling, device_id_type=MESH,
    )

    waits = PLAN["waits"]
    made = 0

    def make_waits(count):
        nonlocal made
        while made < count:
            receive(*waits[made])
            made += 1

    def scores_of(index):
        make_waits(PLAN["before"][index])
        step, unit = units[index]
        if index % per_step == 0:
            prepare(step)
        if index == per_step // 2:
            to_sibling[2].wait_recv()
        return score(step, unit)

    coming = scores_of(0)
    pending = None
    for index, (step, unit) in enumerate(units):
        scores = coming
        if index + 1 < len(units):
            coming = scores_of(index + 1)
        weights, rescale = weigh(unit, scores)
        if pending is not None:
            gather_values(*pending)
        pending = (step, unit, weights, rescale)
        if index == len(units) - per_step // 2:
            finish(1)
            back.start()
    gather_values(*pending)
    finish(0)

    all_parts = items.at[pl.ds(0, 2 * NY - 1)]
    pltpu.make_async_copy(all_parts, all_parts, send_sem).wait()
    for copy in to_sibling:
        copy.wait_send()
    back.wait()


def on_device(queries, keys, values, loader_pos, reset_pos, doc_starts):
    del doc_starts
    bf16, f32 = jnp.bfloat16, jnp.float32
    return pl.pallas_call(
        kernel,
        out_shape=pltpu.VMEM((ROWS, 2 * COLS), bf16),
        in_specs=[pl.BlockSpec(memory_space=pltpu.HBM)] * 5,
        out_specs=pl.BlockSpec(memory_space=pltpu.VMEM),
        scratch_shapes=[
            pltpu.VMEM((2, ROWS, COLS), bf16),
            pltpu.VMEM((2, ROWS, HEAD_WIDTH), bf16),
            pltpu.VMEM((2, ROWS, HEAD_WIDTH), bf16),
            pltpu.VMEM((ROWS,), jnp.int32),
            pltpu.VMEM((ROWS,), jnp.int32),
            pltpu.VMEM((2 * NY, ITEM_ROWS, HEAD_WIDTH), bf16),
            pltpu.VMEM((256, HEAD_WIDTH), bf16),
            pltpu.VMEM((2 * HEAD_WIDTH, 2 * COLS), bf16),
            pltpu.VMEM((HEAD_WIDTH, COLS), bf16),
            pltpu.VMEM((8, ROWS), f32),
            pltpu.VMEM((8, ROWS), f32),
            pltpu.VMEM((2, 8, ROWS), f32),
            pltpu.VMEM((2, 2, 4 * ROWS, ROWS), bf16),
            pltpu.VMEM((1, 2 * COLS), f32),
            pltpu.VMEM((1, 2 * COLS), f32),
            pltpu.VMEM((HEAD_WIDTH, 2 * COLS), f32),
            pltpu.VMEM((ROWS, COLS), bf16),
            pltpu.SemaphoreType.DMA((8,)),
            pltpu.SemaphoreType.DMA((len(PLAN["parts"]), 2 * NY)),
            pltpu.SemaphoreType.DMA((6,)),
            pltpu.SemaphoreType.DMA,
            pltpu.SemaphoreType.DMA((2,)),
        ],
        compiler_params=pltpu.CompilerParams(
            collective_id=0, has_side_effects=True, vmem_limit_bytes=60 * 2**20
        ),
    )(*(pltpu.with_memory_space_constraint(x, pltpu.HBM) for x in (queries, keys, values, loader_pos, reset_pos)))


def solution(mesh):
    rows = ("dp", "ctx")
    return jax.shard_map(
        on_device,
        mesh=mesh,
        in_specs=(P(rows, "tp"), P(rows, "tp"), P(rows, "tp"), P(rows), P(rows), P("dp")),
        out_specs=P(rows, "tp"),
        check_vma=False,
    )
```

```python
import functools
import math

import jax
import jax.numpy as jnp
import numpy as np
from jax import lax
from jax.experimental import pallas as pl
from jax.experimental.pallas import tpu as pltpu
from jax.sharding import PartitionSpec as P

MESH = pl.DeviceIdType.MESH
HEAD_WIDTH = 128
HALF = HEAD_WIDTH // 2
ROPE_BASE = 1000000.0
SCALE = math.log2(math.e) / math.sqrt(HEAD_WIDTH)
ROWS = 128
GROUP = 8
COLS = GROUP * ROWS
NY = 8
UNIT = 512
MASKED = -1e30
ITEM_ROWS = 528

PLAN = {
    "parts": [
        (0, 256), (256, 272),
    ],
    "edges": [
        (0, (-3, 0), (-2, 0)), (0, (-3, 1), (-3, 0)), (0, (-2, 0), (-1, 0)), (0, (-2, 1), (-2, 0)),
        (0, (-1, 0), (0, 0)), (0, (-1, 1), (-1, 0)), (0, (0, 1), (0, 0)), (0, (1, 0), (0, 0)), (0, (1, 1), (1, 0)),
        (0, (2, 0), (1, 0)), (0, (2, 1), (1, 1)), (0, (3, 0), (2, 0)), (0, (3, 1), (3, 0)), (0, (4, 0), (-3, 0)),
        (0, (4, 1), (-3, 1)), (1, (-3, 0), (-2, 0)), (1, (-3, 1), (-3, 0)), (1, (-2, 0), (-1, 0)),
        (1, (-2, 1), (-1, 1)), (1, (-1, 0), (0, 0)), (1, (-1, 1), (-1, 0)), (1, (0, 1), (0, 0)),
        (1, (1, 0), (0, 0)), (1, (1, 1), (0, 1)), (1, (2, 0), (1, 0)), (1, (2, 1), (2, 0)), (1, (3, 0), (2, 0)),
        (1, (3, 1), (2, 1)), (1, (4, 0), (-3, 0)), (1, (4, 1), (4, 0)),
    ],
    "waits": [
        (0, (-1, 0)), (0, (1, 0)), (0, (0, 1)), (1, (-1, 0)), (1, (1, 0)), (1, (0, 1)), (0, (-2, 0)), (0, (-1, 1)),
        (1, (-2, 0)), (0, (1, 1)), (0, (2, 0)), (1, (-1, 1)), (1, (2, 0)), (0, (-3, 0)), (1, (-3, 0)), (1, (1, 1)),
        (0, (-2, 1)), (1, (2, 1)), (0, (2, 1)), (0, (3, 0)), (1, (-2, 1)), (0, (-3, 1)), (0, (4, 0)), (1, (4, 0)),
        (1, (-3, 1)), (1, (3, 0)), (1, (3, 1)), (0, (3, 1)), (0, (4, 1)), (1, (4, 1)),
    ],
    "steps": [
        [(0, 0)], [(-1, 0), (1, 0)], [(0, 1), (-2, 0)], [(-1, 1), (2, 0)], [(-3, 0), (1, 1)], [(2, 1), (-2, 1)],
        [(4, 0), (-3, 1)], [(3, 0), (3, 1)], [(4, 1)],
    ],
    "before": [
        0, 0, 0, 0, 5, 7, 7, 7, 10, 10, 14, 14, 14, 14, 15, 17, 17, 17, 18, 19, 22, 22, 22, 25, 26, 26, 26, 26, 28,
        28, 28, 28, 30, 30, 30, 30,
    ],
}


def sine_cosine(angle):
    turn = jnp.floor(angle * (2.0 / math.pi) + 0.5)
    rest = ((angle - turn * 1.5703125) - turn * 4.837512969970703125e-4) - turn * 7.54978995489188216e-8
    square = rest * rest
    sine = ((-1.9515295891e-4 * square + 8.3321608736e-3) * square - 1.6666654611e-1) * square * rest + rest
    cosine = (
        (2.443315711809948e-5 * square - 1.388731625493765e-3) * square + 4.166664568298827e-2
    ) * square * square - 0.5 * square + 1.0
    quarter = turn.astype(jnp.int32)
    swap = (quarter & 1) == 1
    sine_out = jnp.where(swap, cosine, sine)
    cosine_out = jnp.where(swap, sine, cosine)
    sine_out = jnp.where((quarter & 2) == 2, -sine_out, sine_out)
    cosine_out = jnp.where(((quarter + 1) & 2) == 2, -cosine_out, cosine_out)
    return sine_out, cosine_out


def frequencies():
    row = lax.broadcasted_iota(jnp.int32, (8, ROWS), 0)
    tiles = []
    for first in range(0, HALF, 8):
        tile = jnp.zeros((8, ROWS), jnp.float32)
        for i in range(8):
            tile = jnp.where(row == i, float(np.float32(ROPE_BASE ** (-2.0 * (first + i) / HEAD_WIDTH))), tile)
        tiles.append(tile)
    return jnp.concatenate(tiles, axis=0)


def kernel(
    q_hbm, k_hbm, v_hbm, pos_hbm, reset_hbm, out_ref,
    q_in, k_in, v_in, pos_in, reset_in,
    items, stage, q_t, q_stage, place, place_sib, bounds, mask, top, total, acc, out_buf,
    in_sem, item_sem, sib_sem, send_sem, out_sem,
):
    ctx = lax.axis_index("ctx")
    tp = lax.axis_index("tp")
    dp = lax.axis_index("dp")
    y, z, core = ctx // 4, (ctx // 2) % 2, ctx % 2

    def device(yy, zz, cc):
        return ((yy * 2 + zz) * 2 + cc, tp, dp)

    def around(yy):
        return lax.rem(yy + 2 * NY, NY)

    sibling = device(y, z, 1 - core)

    barrier = pltpu.get_barrier_semaphore()
    strides = set()
    for _, node, parent in PLAN["edges"]:
        stride = ((node[0] - parent[0]) % NY, node[1] ^ parent[1])
        strides |= {stride, (-stride[0] % NY, stride[1])}
    partners = [device(around(y + dy), z if dz == 0 else 1 - z, core) for dy, dz in sorted(strides)] + [sibling]
    for other in partners:
        pl.semaphore_signal(barrier, inc=1, device_id=other, device_id_type=MESH)

    def head_cols(slot, width):
        head = core if slot == 0 else 1 - core
        return pl.ds(pl.multiple_of(head * width, width), width)

    loads = [
        pltpu.make_async_copy(pos_hbm, pos_in, in_sem.at[0]),
        pltpu.make_async_copy(reset_hbm, reset_in, in_sem.at[1]),
    ]
    for slot in (1, 0):
        loads.append(pltpu.make_async_copy(k_hbm.at[:, head_cols(slot, HEAD_WIDTH)], k_in.at[slot], in_sem.at[2 + slot]))
        loads.append(pltpu.make_async_copy(v_hbm.at[:, head_cols(slot, HEAD_WIDTH)], v_in.at[slot], in_sem.at[4 + slot]))
    for slot in (1, 0):
        loads.append(pltpu.make_async_copy(q_hbm.at[:, head_cols(slot, COLS)], q_in.at[slot], in_sem.at[6 + slot]))
    for load in loads:
        load.start()

    for load in loads[:2]:
        load.wait()
    pos = pos_in[...].reshape(1, ROWS).astype(jnp.float32)
    reset = reset_in[...].reshape(1, ROWS).astype(jnp.float32)
    sine, cosine = sine_cosine(frequencies() * reset)
    sine_rows = jnp.concatenate([-sine, sine], axis=0).T
    cosine_rows = jnp.concatenate([cosine, cosine], axis=0).T
    place[...] = jnp.concatenate([pos, pos - reset, jnp.zeros((6, ROWS), jnp.float32)], axis=0)
    bounds[0] = place[...]
    sine_q, cosine_q = sine * SCALE, cosine * SCALE

    my_slot = y * 2 + z
    for load in loads[2:6]:
        load.wait()

    def keys_of(slot):
        raw = k_in[slot].astype(jnp.float32)
        return (raw * cosine_rows + pltpu.roll(raw, HALF, 1) * sine_rows).astype(jnp.bfloat16)

    def values_of(slot):
        return v_in[slot].astype(jnp.float32).T.astype(jnp.bfloat16)

    stage[0:ROWS] = keys_of(1)
    stage[ROWS : 2 * ROWS] = values_of(1)
    items[my_slot, 0:ROWS] = keys_of(0)
    items[my_slot, ROWS : 2 * ROWS] = values_of(0)

    unit_matrix = (
        lax.broadcasted_iota(jnp.int32, (ROWS, ROWS), 0) == lax.broadcasted_iota(jnp.int32, (ROWS, ROWS), 1)
    ).astype(jnp.float32).astype(jnp.bfloat16)
    for head in range(2 * GROUP):
        q_t[HEAD_WIDTH:, head * ROWS : (head + 1) * ROWS] = unit_matrix
    top[...] = jnp.full_like(top, MASKED)
    total[...] = jnp.zeros_like(total)
    acc[...] = jnp.zeros_like(acc)

    pl.semaphore_wait(barrier, len(partners))

    to_sibling = [
        pltpu.make_async_remote_copy(
            src_ref=place, dst_ref=place_sib, send_sem=sib_sem.at[0], recv_sem=sib_sem.at[1],
            device_id=sibling, device_id_type=MESH,
        ),
        pltpu.make_async_remote_copy(
            src_ref=stage, dst_ref=items.at[my_slot, pl.ds(256, 256)], send_sem=sib_sem.at[2],
            recv_sem=sib_sem.at[3], device_id=sibling, device_id_type=MESH,
        ),
        pltpu.make_async_remote_copy(
            src_ref=q_stage, dst_ref=q_t.at[pl.ds(0, HEAD_WIDTH), pl.ds(COLS, COLS)], send_sem=sib_sem.at[4],
            recv_sem=sib_sem.at[5], device_id=sibling, device_id_type=MESH,
        ),
    ]

    def part_copy(sub, slot, target):
        rows = items.at[slot, pl.ds(*PLAN["parts"][sub])]
        return pltpu.make_async_remote_copy(
            src_ref=rows, dst_ref=rows, send_sem=send_sem, recv_sem=item_sem.at[sub, slot],
            device_id=target, device_id_type=MESH,
        )

    children = {}
    for sub, node, parent in PLAN["edges"]:
        children.setdefault((sub, parent), []).append(node)

    def slot_of(node):
        return around(y - node[0]) * 2 + (z if node[1] == 0 else 1 - z)

    def hand_on(sub, node):
        for child in children.get((sub, node), []):
            target = device(around(y + child[0] - node[0]), z if child[1] == node[1] else 1 - z, core)
            part_copy(sub, slot_of(node), target).start()

    def receive(sub, node):
        part_copy(sub, slot_of(node), sibling).wait_recv()
        hand_on(sub, node)

    def rotate_queries(slot):
        for head in range(GROUP):
            cols = slice(head * ROWS, (head + 1) * ROWS)
            raw = q_in[slot, :, cols].astype(jnp.float32).T
            low, high = raw[:HALF], raw[HALF:]
            turned = jnp.concatenate(
                [low * cosine_q - high * sine_q, high * cosine_q + low * sine_q], axis=0
            ).astype(jnp.bfloat16)
            if slot == 0:
                q_t[0:HEAD_WIDTH, cols] = turned
            else:
                q_stage[:, cols] = turned

    to_sibling[0].start()
    to_sibling[1].start()
    for part, (first, _) in enumerate(PLAN["parts"]):
        if first < 256:
            hand_on(part, (0, 0))
    loads[7].wait()
    rotate_queries(0)

    to_sibling[0].wait_recv()
    bounds[1] = place_sib[...]
    place_rows = []
    for group in range(2):
        at = bounds[group, 0:1]
        high = jnp.floor(at * (1.0 / 64.0))
        place_rows += [high, at - high * 64.0]
    items[my_slot, 512:528] = jnp.concatenate(
        place_rows + [jnp.zeros((12, ROWS), jnp.float32)], axis=0
    ).astype(jnp.bfloat16)
    to_sibling[1].wait_recv()
    for part, (first, _) in enumerate(PLAN["parts"]):
        if first >= 256:
            hand_on(part, (0, 0))

    loads[6].wait()
    rotate_queries(1)
    to_sibling[2].start()
    steps = PLAN["steps"]
    per_step = 2 * COLS // UNIT
    units = [(0, unit) for unit in range(per_step)]
    units += [(step, unit) for step in range(1, len(steps)) for unit in reversed(range(per_step))]

    def prepare(step):
        row = 0
        for node in steps[step]:
            slot = slot_of(node)
            tile = items[slot, 512:528].astype(jnp.float32)
            for part in range(2):
                at = tile[2 * part : 2 * part + 1] * 64.0 + tile[2 * part + 1 : 2 * part + 2]
                at = jnp.broadcast_to(at, (ROWS, ROWS)).T
                for group in range(2):
                    seen = (at <= bounds[group, 0:1]) & (at >= bounds[group, 1:2])
                    mask[step % 2, group, row : row + ROWS] = jnp.where(seen, 0.0, MASKED).astype(jnp.bfloat16)
                row += ROWS

    def score(step, unit):
        group = unit * UNIT // COLS
        keys = []
        for node in steps[step]:
            slot = slot_of(node)
            keys += [items[slot, 0:ROWS], items[slot, 256 : 256 + ROWS]]
        keys = jnp.concatenate(keys, axis=0)
        left = jnp.concatenate([keys, mask[step % 2, group, : keys.shape[0]]], axis=1)
        return jnp.dot(left, q_t[:, unit * UNIT : (unit + 1) * UNIT], preferred_element_type=jnp.float32)

    def weigh(unit, scores):
        cols = slice(unit * UNIT, (unit + 1) * UNIT)
        before = top[:, cols]
        now = jnp.maximum(before, jnp.max(scores, axis=0, keepdims=True))
        rescale = jnp.exp2(before - now)
        top[:, cols] = now
        weights = jnp.exp2(scores - now)
        total[:, cols] = total[:, cols] * rescale + jnp.sum(weights, axis=0, keepdims=True)
        return weights.astype(jnp.bfloat16), rescale

    def gather_values(step, unit, weights, rescale):
        cols = slice(unit * UNIT, (unit + 1) * UNIT)
        values = []
        for node in steps[step]:
            slot = slot_of(node)
            values += [items[slot, ROWS : 2 * ROWS], items[slot, 256 + ROWS : 512]]
        values = jnp.concatenate(values, axis=1)
        acc[:, cols] = acc[:, cols] * rescale + jnp.dot(values, weights, preferred_element_type=jnp.float32)

    def finish(group):
        for head in range(GROUP):
            cols = slice(group * COLS + head * ROWS, group * COLS + (head + 1) * ROWS)
            result = (acc[:, cols] / total[:, cols]).T.astype(jnp.bfloat16)
            if group == 0:
                out_ref[:, pl.ds(pl.multiple_of(core * COLS + head * ROWS, ROWS), ROWS)] = result
            else:
                out_buf[:, head * ROWS : (head + 1) * ROWS] = result

    back = pltpu.make_async_remote_copy(
        src_ref=out_buf, dst_ref=out_ref.at[:, pl.ds(pl.multiple_of(core * COLS, COLS), COLS)],
        send_sem=out_sem.at[0], recv_sem=out_sem.at[1], device_id=sibling, device_id_type=MESH,
    )

    waits = PLAN["waits"]
    made = 0

    def make_waits(count):
        nonlocal made
        while made < count:
            receive(*waits[made])
            made += 1

    def scores_of(index):
        make_waits(PLAN["before"][index])
        step, unit = units[index]
        if index % per_step == 0:
            prepare(step)
        if index == per_step // 2:
            to_sibling[2].wait_recv()
        return score(step, unit)

    coming = scores_of(0)
    pending = None
    for index, (step, unit) in enumerate(units):
        scores = coming
        if index + 1 < len(units):
            coming = scores_of(index + 1)
        weights, rescale = weigh(unit, scores)
        if pending is not None:
            gather_values(*pending)
        pending = (step, unit, weights, rescale)
        if index == len(units) - per_step // 2:
            finish(1)
            back.start()
    gather_values(*pending)
    finish(0)

    all_parts = items.at[pl.ds(0, 2 * NY - 1)]
    pltpu.make_async_copy(all_parts, all_parts, send_sem).wait()
    for copy in to_sibling:
        copy.wait_send()
    back.wait()


def on_device(queries, keys, values, loader_pos, reset_pos, doc_starts):
    del doc_starts
    bf16, f32 = jnp.bfloat16, jnp.float32
    return pl.pallas_call(
        kernel,
        out_shape=pltpu.VMEM((ROWS, 2 * COLS), bf16),
        in_specs=[pl.BlockSpec(memory_space=pltpu.HBM)] * 5,
        out_specs=pl.BlockSpec(memory_space=pltpu.VMEM),
        scratch_shapes=[
            pltpu.VMEM((2, ROWS, COLS), bf16),
            pltpu.VMEM((2, ROWS, HEAD_WIDTH), bf16),
            pltpu.VMEM((2, ROWS, HEAD_WIDTH), bf16),
            pltpu.VMEM((ROWS,), jnp.int32),
            pltpu.VMEM((ROWS,), jnp.int32),
            pltpu.VMEM((2 * NY, ITEM_ROWS, HEAD_WIDTH), bf16),
            pltpu.VMEM((256, HEAD_WIDTH), bf16),
            pltpu.VMEM((2 * HEAD_WIDTH, 2 * COLS), bf16),
            pltpu.VMEM((HEAD_WIDTH, COLS), bf16),
            pltpu.VMEM((8, ROWS), f32),
            pltpu.VMEM((8, ROWS), f32),
            pltpu.VMEM((2, 8, ROWS), f32),
            pltpu.VMEM((2, 2, 4 * ROWS, ROWS), bf16),
            pltpu.VMEM((1, 2 * COLS), f32),
            pltpu.VMEM((1, 2 * COLS), f32),
            pltpu.VMEM((HEAD_WIDTH, 2 * COLS), f32),
            pltpu.VMEM((ROWS, COLS), bf16),
            pltpu.SemaphoreType.DMA((8,)),
            pltpu.SemaphoreType.DMA((len(PLAN["parts"]), 2 * NY)),
            pltpu.SemaphoreType.DMA((6,)),
            pltpu.SemaphoreType.DMA,
            pltpu.SemaphoreType.DMA((2,)),
        ],
        compiler_params=pltpu.CompilerParams(
            collective_id=0, has_side_effects=True, vmem_limit_bytes=60 * 2**20
        ),
    )(*(pltpu.with_memory_space_constraint(x, pltpu.HBM) for x in (queries, keys, values, loader_pos, reset_pos)))


def solution(mesh):
    rows = ("dp", "ctx")
    return jax.shard_map(
        on_device,
        mesh=mesh,
        in_specs=(P(rows, "tp"), P(rows, "tp"), P(rows, "tp"), P(rows), P(rows), P("dp")),
        out_specs=P(rows, "tp"),
        check_vma=False,
    )
```
